32 devices in a mesh: group: 2 (over x), dp: 16 (over z, y, core).
Axes of the slice: x: 2, y: 2, z: 4, core: 2. Of those that a mesh axis runs over, the one named last changes fastest.
Arguments:
- inputs: bfloat16 [4096, 8192], P(('group', 'dp')), parts along dimension 0, may hold values from -6 to 6
- pack_dest: int32 [4096], P(('group', 'dp')), parts along dimension 0, may hold values from 0 to 2047, as said below
- row_adapter: int32 [4096], P(('group', 'dp')), parts along dimension 0, may hold values from 0 to 7, as said below
- value_matrix: bfloat16 [8192, 1024], P('dp'), may hold values from -0.0625 to 0.0625
- down_master: float32 [16384, 128], P(('group', 'dp')), parts along dimension 0, may hold values from -0.0625 to 0.0625
- up_master: float32 [256, 1024], P(('group', 'dp')), parts along dimension 0, may hold values from -1.5 to 1.5
- down_m: float32 [16384, 128], P(('group', 'dp')), parts along dimension 0, may hold values from -0.24 to 0.24
- down_v: float32 [16384, 128], P(('group', 'dp')), parts along dimension 0, may hold values from 0.0005 to 0.005
- up_m: float32 [256, 1024], P(('group', 'dp')), parts along dimension 0, may hold values from -0.03 to 0.03
- up_v: float32 [256, 1024], P(('group', 'dp')), parts along dimension 0, may hold values from 1e-05 to 0.0001
- value_gradient: bfloat16 [4096, 1024], P(('group', 'dp')), parts along dimension 0, may hold values from -6 to 6
Outputs:
- values: bfloat16 [4096, 1024], P(('group', 'dp')), parts along dimension 0
- input_gradient: bfloat16 [4096, 8192], P(('group', 'dp')), parts along dimension 0
- new_down: float32 [16384, 128], P(('group', 'dp')), parts along dimension 0
- new_down_m: float32 [16384, 128], P(('group', 'dp')), parts along dimension 0
- new_down_v: float32 [16384, 128], P(('group', 'dp')), parts along dimension 0
- new_up: float32 [256, 1024], P(('group', 'dp')), parts along dimension 0
- new_up_m: float32 [256, 1024], P(('group', 'dp')), parts along dimension 0
- new_up_v: float32 [256, 1024], P(('group', 'dp')), parts along dimension 0
The draws below stay inside these ranges and needn't reach their ends.
There are 2 independent parts, one for each index of `group`. The reference program is written for one: setup_inputs(seed, part) draws one part's arguments, and reference() takes and returns one part's arrays. A program takes and returns all parts, laid end to end along the dimension named above; an argument that names none is the same for every part. Nothing has to cross between parts.
Inputs may be any that keep to these rules, and one draw needn't show every extreme that they name: pack_dest is a permutation of the rows; the 128 rows of each device go to exactly 8 packed positions on each device, position d * 128 to (d + 1) * 128 - 1 being device d's. row_adapter is constant over runs of packed rows (sequences).
All inputs are finite; a program needn't handle non-finite values.
Results may differ from the reference program's by a relative error of at most 0.0061.
Values may be sent and summed in bfloat16 or wider, within the bound.
A program may use at most 128 MiB of HBM per device.

```python
import math
import jax
import jax.numpy as jnp

D = 8192
DV = 1024
RANK = 16
ADAPTERS = 8
TOK_DEV = 128
TOTAL_TOKEN_ROWS = 2048


def draw_pack_dest(key, part):
    key = jax.random.fold_in(key, 11)
    key_src, key_dst = jax.random.split(key)
    blocks = TOTAL_TOKEN_ROWS // TOK_DEV
    per_peer = TOK_DEV // blocks
    lanes = jax.vmap(lambda sub: jax.random.permutation(sub, TOK_DEV))(jax.random.split(key_src, blocks)).astype(jnp.int32)
    spots = jax.vmap(lambda sub: jax.random.permutation(sub, TOK_DEV))(jax.random.split(key_dst, blocks)).astype(jnp.int32)
    target = lanes // per_peer
    within = lanes % per_peer
    source = jnp.arange(blocks, dtype=jnp.int32)[:, None]
    landing = spots[target, source * per_peer + within]
    return (target * TOK_DEV + landing).reshape(TOTAL_TOKEN_ROWS).astype(jnp.int32)


def draw_row_adapter(key, part):
    key = jax.random.fold_in(key, 7)
    key_start, key_table = jax.random.split(key)
    starts = (jax.random.randint(key_start, (TOTAL_TOKEN_ROWS,), 0, 32) == 0).astype(jnp.int32)
    segment = jnp.cumsum(starts).astype(jnp.int32)
    table = jax.random.randint(key_table, (TOTAL_TOKEN_ROWS + 1,), 0, ADAPTERS).astype(jnp.int32)
    return table[segment]


def shard_levels(own_key, shape, cuts, smallest, top_value):
    def one(position, blocks):
        heights = jax.random.uniform(jax.random.fold_in(jax.random.fold_in(own_key, 6), position), (blocks,), jnp.float32, smallest / len(cuts), top_value / len(cuts))
        return jnp.repeat(jnp.exp(heights), shape[position] // blocks).reshape((-1,) + (1,) * (len(shape) - position - 1))

    gain = one(*cuts[0])
    for cut in cuts[1:]:
        gain = gain * one(*cut)
    return gain


def scatter_about(stream_key, shape, width, bound, shards=(), kind=jnp.bfloat16):
    entries = width * jax.random.normal(stream_key, shape, jnp.float32)
    if shards:
        entries = entries * shard_levels(stream_key, shape, shards, -0.22, 0.18)
    return jnp.clip(entries, -bound, bound).astype(kind)


def setup_inputs(seed: int = 0, part: int = 0) -> dict:
    seeds = jax.random.split(jax.random.key(seed), 12)
    part_splits = jax.random.split(jax.random.fold_in(seeds[11], part), 12)
    return {
        "inputs": scatter_about(part_splits[0], (TOTAL_TOKEN_ROWS, D), 1.0, 6.0, ((0, 16),)),
        "pack_dest": draw_pack_dest(jax.random.fold_in(jax.random.fold_in(seeds[11], part), 71), part),
        "row_adapter": draw_row_adapter(jax.random.fold_in(jax.random.fold_in(seeds[11], part), 71), part),
        "value_matrix": scatter_about(seeds[3], (D, DV), D ** -0.5, 0.0625, ((0, 16),)),
        "down_master": scatter_about(part_splits[4], (D, ADAPTERS * RANK), D ** -0.5, 0.0625, ((0, 16),), jnp.float32),
        "up_master": scatter_about(part_splits[5], (ADAPTERS * RANK, DV), RANK ** -0.5, 1.5, ((0, 16),), jnp.float32),
        "down_m": scatter_about(part_splits[6], (D, ADAPTERS * RANK), 0.04, 0.24, ((0, 16),), jnp.float32),
        "down_v": jnp.clip(jnp.exp(math.log(0.005) - 2.30258502 * jax.random.uniform(part_splits[7], (D, ADAPTERS * RANK), jnp.float32) ** shard_levels(part_splits[7], (D, ADAPTERS * RANK), ((0, 16),), -0.2, 0.2)), 0.0005, 0.005),
        "up_m": scatter_about(part_splits[8], (ADAPTERS * RANK, DV), 0.005, 0.03, ((0, 16),), jnp.float32),
        "up_v": jnp.clip(jnp.exp(math.log(0.0001) - 2.3025851 * jax.random.uniform(part_splits[9], (ADAPTERS * RANK, DV), jnp.float32) ** shard_levels(part_splits[9], (ADAPTERS * RANK, DV), ((0, 16),), -0.2, 0.2)), 9.999999747378752e-06, 0.0001),
        "value_gradient": scatter_about(part_splits[10], (TOTAL_TOKEN_ROWS, DV), 1.0, 6.0, ((0, 16),)),
    }


adapter_scale = 2.0
beta_one = 0.9
beta_two = 0.999
learn_rate = 0.001
adam_eps = 1e-08
first_fix = 1.0 - 0.9 ** 10
second_fix = 1.0 - 0.999 ** 10

def adam_update(param, moment, second, gradient):
    moment_new = beta_one * moment + (1.0 - beta_one) * gradient
    second_new = beta_two * second + (1.0 - beta_two) * gradient * gradient
    param_new = param - learn_rate * (moment_new / first_fix) / (jnp.sqrt(second_new / second_fix) + adam_eps)
    return (param_new, moment_new, second_new)

def reference(inputs, pack_dest, row_adapter, value_matrix, down_master, up_master, down_m, down_v, up_m, up_v, value_gradient):
    packed_rows = jnp.zeros_like(inputs).at[pack_dest].set(inputs)
    down_batched = down_master.astype(jnp.bfloat16)
    up_batched = up_master.astype(jnp.bfloat16)
    columns = ADAPTERS * RANK
    owners = (jnp.arange(columns).astype(jnp.int32) // RANK).astype(jnp.int32)
    chosen = row_adapter[:, None] == owners[None, :]
    low_rank_term = jnp.where(chosen, jnp.dot(packed_rows, down_batched, preferred_element_type=jnp.float32), 0.0).astype(jnp.bfloat16)
    backward_pass = jnp.where(chosen, jnp.dot(value_gradient, up_batched.T, preferred_element_type=jnp.float32), 0.0).astype(jnp.bfloat16)
    values = jnp.dot(packed_rows, value_matrix, preferred_element_type=jnp.float32) + adapter_scale * jnp.dot(low_rank_term, up_batched, preferred_element_type=jnp.float32)
    input_gradient = jnp.dot(value_gradient, value_matrix.T, preferred_element_type=jnp.float32) + adapter_scale * jnp.dot(backward_pass, down_batched.T, preferred_element_type=jnp.float32)
    scale_factor = adapter_scale / TOTAL_TOKEN_ROWS
    grad_down = jnp.dot(packed_rows.T, backward_pass, preferred_element_type=jnp.float32) * scale_factor
    grad_up = jnp.dot(low_rank_term.T, value_gradient, preferred_element_type=jnp.float32) * scale_factor
    new_down, new_down_m, new_down_v = adam_update(down_master, down_m, down_v, grad_down)
    new_up, new_up_m, new_up_v = adam_update(up_master, up_m, up_v, grad_up)
    return (values.astype(jnp.bfloat16), input_gradient.astype(jnp.bfloat16), new_down, new_down_m, new_down_v, new_up, new_up_m, new_up_v)
```

```python
import functools

import jax
import jax.numpy as jnp
from jax import lax
from jax.experimental import pallas as pl
from jax.experimental.pallas import tpu as pltpu
from jax.sharding import PartitionSpec as P

RANK = 16
PAD = 16
MESH = pl.DeviceIdType.MESH

adapter_scale = 2.0
beta_one = 0.9
beta_two = 0.999
learn_rate = 0.001
adam_eps = 1e-08
first_fix = 1.0 - 0.9**10
second_fix = 1.0 - 0.999**10

bf16, f32, i32 = jnp.bfloat16, jnp.float32, jnp.int32


def adam_update(param, moment, second, gradient):
    moment_new = beta_one * moment + (1.0 - beta_one) * gradient
    second_new = beta_two * second + (1.0 - beta_two) * gradient * gradient
    param_new = param - learn_rate * (moment_new / first_fix) / (
        jnp.sqrt(second_new / second_fix) + adam_eps
    )
    return (param_new, moment_new, second_new)


def dot(left, right, lc=1, rc=0):
    return lax.dot_general(
        left, right, (((lc,), (rc,)), ((), ())), preferred_element_type=f32
    )


def iota(shape, dim):
    return lax.broadcasted_iota(i32, shape, dim)


def onehot(cond):
    return jnp.where(cond, 1.0, 0.0).astype(bf16)


def kernel(
    n,
    up_rows,
    x_ref,
    pd_col_ref,
    pd_row_ref,
    ra_col_ref,
    wd_ref,
    upad_ref,
    dv_ref,
    values_ref,
    ig_ref,
    gd_ref,
    gu_ref,
    wd_all,
    up_all,
    b_all,
    g_send,
    g_recv,
    v_send,
    v_recv,
    u_send,
    u_recv,
    acc,
    dvb,
    ring_send,
    ring_recv,
    sib_send,
    sib_recv,
    push_send,
    push_recv,
):
    tok = x_ref.shape[0]
    depth, wide = wd_ref.shape
    dv_width = dv_ref.shape[1]
    cols = wide - dv_width
    chips = n // 2
    half = depth // 2
    me = lax.axis_index("dp")
    core = lax.rem(me, 2)
    chip = me // 2
    zs = chips // 2

    def place_of(c):
        z, y = c // 2, lax.rem(c, 2)
        return jnp.where(y == 0, z, chips - 1 - z)

    def chip_at(p):
        p = lax.rem(p + chips, chips)
        return jnp.where(p < zs, 2 * p, 2 * (chips - 1 - p) + 1)

    place = place_of(chip)
    sibling = 2 * chip + 1 - core

    barrier = pltpu.get_barrier_semaphore()

    @pl.loop(1, n)
    def _(j):
        pl.semaphore_signal(
            barrier, inc=1, device_id={"dp": lax.rem(me + j, n)}, device_id_type=MESH
        )

    pl.semaphore_wait(barrier, n - 1)

    def push(phase, j, src, dst):
        return pltpu.make_async_remote_copy(
            src_ref=src,
            dst_ref=dst,
            send_sem=push_send.at[phase, j],
            recv_sem=push_recv.at[phase, j],
            device_id={"dp": lax.rem(me + j, n)},
            device_id_type=MESH,
        )

    def push_all(phase, src_of, dst):
        @pl.loop(1, n)
        def _(j):
            push(phase, j, src_of(lax.rem(me + j, n)), dst).start()

    def wait_all(phase, src_of, dst):
        @pl.loop(1, n)
        def _(j):
            push(phase, j, src_of(lax.rem(me + j, n)), dst).wait()

    last = chips // 2

    def part_of(idx, step, way):
        if step < last:
            return wd_all.at[idx]
        return wd_all.at[idx, pl.ds(way * half, half)]

    def source_place(step, way):
        return place - step if way == 0 else place + step

    def ring(step, way):
        target = place + 1 if way == 0 else place - 1
        origin = 2 * chip_at(source_place(step - 1, way)) + core
        return pltpu.make_async_remote_copy(
            src_ref=part_of(origin, step, way),
            dst_ref=part_of(origin, step, way),
            send_sem=ring_send.at[way, step],
            recv_sem=ring_recv.at[way, step],
            device_id={"dp": 2 * chip_at(target) + core},
            device_id_type=MESH,
        )

    def sib(step, way):
        origin = 2 * chip_at(source_place(step, way)) + core
        return pltpu.make_async_remote_copy(
            src_ref=part_of(origin, step, way),
            dst_ref=part_of(origin, step, way),
            send_sem=sib_send.at[way, step],
            recv_sem=sib_recv.at[way, step],
            device_id={"dp": sibling},
            device_id_type=MESH,
        )

    up_all[me] = upad_ref[...]
    push_all(0, lambda d: upad_ref, up_all.at[me])
    wd_all[me] = wd_ref[...]
    ring(1, 0).start()
    ring(1, 1).start()
    sib(0, 0).start()
    wait_all(0, lambda d: upad_ref, up_all.at[me])

    up_flat = up_all[...].reshape(n * PAD, dv_width)
    q = iota((cols, n * PAD), 1)
    r = iota((cols, n * PAD), 0)
    spread = onehot((q % PAD < up_rows) & ((q // PAD) * up_rows + q % PAD == r))
    up_full = dot(spread, up_flat).astype(bf16)
    owner = iota((tok, cols), 1) // RANK
    back = dot(dv_ref[...], up_full, 1, 1)
    back = jnp.where(ra_col_ref[...] == owner, back, 0.0).astype(bf16)
    b_all[me] = back
    push_all(1, lambda d: b_all.at[me], b_all.at[me])
    dvb[:, :dv_width] = dv_ref[...]
    dvb[:, dv_width:] = (back.astype(f32) * adapter_scale).astype(bf16)
    acc[...] = jnp.zeros_like(acc)

    def work(p, k):
        d = 2 * chip_at(p) + k
        where = pl.ds(pl.multiple_of(d * depth, depth), depth)
        block = wd_all[d]
        acc[...] += dot(x_ref[:, where], block)
        ig_ref[:, where] = dot(dvb[...], block, 1, 1).astype(bf16)

    def step_on(step):
        for way in (0, 1):
            ring(step, way).wait_recv()
            if step < last:
                ring(step + 1, way).start()
            sib(step, way).start()

    step_on(1)
    work(place, core)

    wait_all(1, lambda d: b_all.at[me], b_all.at[me])
    pd_col = pd_col_ref[...]

    def pick(d, carry):
        rows, adapter = carry
        hit = pd_col == d * tok + iota((tok, tok), 1)
        rows = rows + dot(onehot(hit), b_all[d])
        ad = up_all[d][up_rows : up_rows + 1, :tok].astype(f32)
        adapter = adapter + jnp.sum(jnp.where(hit, ad, 0.0), axis=1, keepdims=True)
        return rows, adapter

    home, adapter = lax.fori_loop(
        0, n, pick, (jnp.zeros((tok, cols), f32), jnp.zeros((tok, 1), f32))
    )
    home = home.astype(bf16)
    scale_factor = adapter_scale / (tok * n)

    @pl.loop(0, n)
    def _(d):
        where = pl.ds(pl.multiple_of(d * depth, depth), depth)
        g_send[d] = (dot(x_ref[:, where], home, 0, 0) * scale_factor).astype(bf16)

    push_all(2, lambda d: g_send.at[d], g_recv.at[me])
    g_recv[me] = g_send[me]

    sib(0, 0).wait_recv()
    work(place, 1 - core)
    for step in range(2, last + 1):
        step_on(step)
        for way in (0, 1):
            work(source_place(step - 1, way), core)
            sib(step - 1, way).wait_recv()
            work(source_place(step - 1, way), 1 - core)
    work(place + last, core)
    sib(last, 0).wait_recv()
    sib(last, 1).wait_recv()
    work(place + last, 1 - core)

    low = jnp.where(adapter == owner.astype(f32), acc[:, dv_width:], 0.0).astype(bf16)
    val = (acc[:, :dv_width] + adapter_scale * dot(low, up_full)).astype(bf16)
    tr = pd_row_ref[...] // tok
    same = (pd_col // tok == tr) & (iota((tok, tok), 0) < iota((tok, tok), 1))
    turn = jnp.sum(jnp.where(same, 1.0, 0.0), axis=0, keepdims=True).astype(i32)
    order = onehot(tr * PAD + turn == iota((n * PAD, tok), 0))
    slot = jnp.broadcast_to((pd_col % tok + 1).astype(f32), (tok, tok)).astype(bf16)
    for part, lo, hi in (
        (val, 0, dv_width),
        (low, dv_width, wide),
        (slot, wide, wide + tok),
    ):
        v_send[:, :, lo:hi] = dot(order, part).astype(bf16).reshape(n, PAD, hi - lo)
    push_all(3, lambda d: v_send.at[d], v_recv.at[me])
    v_recv[me] = v_send[me]

    wait_all(2, lambda d: g_send.at[d], g_recv.at[me])
    gd_ref[...] = lax.fori_loop(
        0, n, lambda d, s: s + g_recv[d].astype(f32), jnp.zeros(gd_ref.shape, f32)
    )

    wait_all(3, lambda d: v_send.at[d], v_recv.at[me])
    got = v_recv[...].reshape(n * PAD, wide + tok)
    put = onehot(got[:, wide:].astype(f32) == (iota((n * PAD, tok), 1) + 1).astype(f32))
    packed = dot(put, got[:, :wide], 0, 0).astype(bf16)
    values_ref[...] = packed[:, :dv_width]

    low_wide = dot(packed[:, dv_width:], spread).astype(bf16)
    grad_up = dot(low_wide, dv_ref[...], 0, 0) * scale_factor
    u_send[...] = grad_up.astype(bf16).reshape(n, PAD, dv_width)
    push_all(4, lambda d: u_send.at[d], u_recv.at[me])
    u_recv[me] = u_send[me]

    for way in (0, 1):
        for step in range(1, last + 1):
            ring(step, way).wait_send()
            sib(step, way).wait_send()
    sib(0, 0).wait_send()

    wait_all(4, lambda d: u_send.at[d], u_recv.at[me])
    gu_ref[...] = lax.fori_loop(
        0, n, lambda d, s: s + u_recv[d].astype(f32), jnp.zeros(gu_ref.shape, f32)
    )


def local(
    n,
    inputs,
    pack_dest,
    row_adapter,
    value_matrix,
    down_master,
    up_master,
    down_m,
    down_v,
    up_m,
    up_v,
    value_gradient,
):
    tok, width = inputs.shape
    depth, dv_width = value_matrix.shape
    cols = down_master.shape[1]
    up_rows = up_master.shape[0]
    wide = dv_width + cols
    wd = jnp.concatenate([value_matrix, down_master.astype(bf16)], axis=1)
    upad = jnp.zeros((PAD, dv_width), bf16)
    upad = upad.at[:up_rows].set(up_master.astype(bf16))
    upad = upad.at[up_rows, :tok].set(row_adapter.astype(bf16))
    steps = n // 4 + 1
    vmem = pl.BlockSpec(memory_space=pltpu.VMEM)
    values, input_gradient, grad_down, grad_up = pl.pallas_call(
        functools.partial(kernel, n, up_rows),
        out_shape=(
            jax.ShapeDtypeStruct((tok, dv_width), bf16),
            jax.ShapeDtypeStruct((tok, width), bf16),
            jax.ShapeDtypeStruct((depth, cols), f32),
            jax.ShapeDtypeStruct((PAD, dv_width), f32),
        ),
        in_specs=[vmem] * 7,
        out_specs=[vmem] * 4,
        scratch_shapes=[
            pltpu.VMEM((n, depth, wide), bf16),
            pltpu.VMEM((n, PAD, dv_width), bf16),
            pltpu.VMEM((n, tok, cols), bf16),
            pltpu.VMEM((n, depth, cols), bf16),
            pltpu.VMEM((n, depth, cols), bf16),
            pltpu.VMEM((n, PAD, wide + tok), bf16),
            pltpu.VMEM((n, PAD, wide + tok), bf16),
            pltpu.VMEM((n, PAD, dv_width), bf16),
            pltpu.VMEM((n, PAD, dv_width), bf16),
            pltpu.VMEM((tok, wide), f32),
            pltpu.VMEM((tok, wide), bf16),
            pltpu.SemaphoreType.DMA((2, steps)),
            pltpu.SemaphoreType.DMA((2, steps)),
            pltpu.SemaphoreType.DMA((2, steps)),
            pltpu.SemaphoreType.DMA((2, steps)),
            pltpu.SemaphoreType.DMA((5, n)),
            pltpu.SemaphoreType.DMA((5, n)),
        ],
        compiler_params=pltpu.CompilerParams(
            collective_id=0, has_side_effects=True, vmem_limit_bytes=56 * 2**20
        ),
        cost_estimate=pl.CostEstimate(
            flops=6 * tok * width * wide,
            bytes_accessed=2 * (2 * tok * width + width * wide),
            transcendentals=0,
        ),
    )(
        inputs,
        pack_dest.reshape(tok, 1),
        pack_dest.reshape(1, tok),
        row_adapter.reshape(tok, 1),
        wd,
        upad,
        value_gradient,
    )
    new_down, new_down_m, new_down_v = adam_update(down_master, down_m, down_v, grad_down)
    new_up, new_up_m, new_up_v = adam_update(up_master, up_m, up_v, grad_up[:up_rows])
    return (values, input_gradient, new_down, new_down_m, new_down_v, new_up, new_up_m, new_up_v)


def solution(mesh):
    both = P(("group", "dp"), None)
    line = P(("group", "dp"))
    in_specs = (both, line, line, P("dp", None)) + (both,) * 7
    return jax.shard_map(
        functools.partial(local, mesh.shape["dp"]),
        mesh=mesh,
        in_specs=in_specs,
        out_specs=(both,) * 8,
        check_vma=False,
    )
```

```python
import functools

import jax
import jax.numpy as jnp
from jax import lax
from jax.experimental import pallas as pl
from jax.experimental.pallas import tpu as pltpu
from jax.sharding import PartitionSpec as P

RANK = 16
PAD = 16
SIDE = PAD // 2
MESH = pl.DeviceIdType.MESH

adapter_scale = 2.0
beta_one = 0.9
beta_two = 0.999
learn_rate = 0.001
adam_eps = 1e-08
first_fix = 1.0 - 0.9**10
second_fix = 1.0 - 0.999**10

bf16, f32, i32 = jnp.bfloat16, jnp.float32, jnp.int32


def adam_update(param, moment, second, gradient):
    moment_new = beta_one * moment + (1.0 - beta_one) * gradient
    second_new = beta_two * second + (1.0 - beta_two) * gradient * gradient
    param_new = param - learn_rate * (moment_new / first_fix) / (
        jnp.sqrt(second_new / second_fix) + adam_eps
    )
    return (param_new, moment_new, second_new)


def dot(left, right, lc=1, rc=0):
    return lax.dot_general(
        left, right, (((lc,), (rc,)), ((), ())), preferred_element_type=f32
    )


def iota(shape, dim):
    return lax.broadcasted_iota(i32, shape, dim)


def onehot(cond):
    return jnp.where(cond, 1.0, 0.0).astype(bf16)


def kernel(
    n,
    up_rows,
    x_ref,
    pd_col_ref,
    pd_row_ref,
    ra_col_ref,
    wd_ref,
    upad_ref,
    dv_ref,
    values_ref,
    ig_ref,
    gd_ref,
    gu_ref,
    wd_all,
    up_all,
    b_all,
    grad,
    grad_core,
    grad_y,
    grad_z,
    v_send,
    v_recv,
    u_send,
    u_recv,
    acc,
    dvb,
    ring_send,
    ring_recv,
    sib_send,
    sib_recv,
    push_send,
    push_recv,
    pair_send,
    pair_recv,
    z_send,
    z_recv,
):
    tok = x_ref.shape[0]
    depth, wide = wd_ref.shape
    dv_width = dv_ref.shape[1]
    cols = wide - dv_width
    chips = n // 2
    half = depth // 2
    me = lax.axis_index("dp")
    core = lax.rem(me, 2)
    chip = me // 2
    zs = chips // 2
    my_z, my_y = chip // 2, lax.rem(chip, 2)
    left = dv_width // 2

    def place_of(c):
        z, y = c // 2, lax.rem(c, 2)
        return jnp.where(y == 0, z, chips - 1 - z)

    def chip_at(p):
        p = lax.rem(p + chips, chips)
        return jnp.where(p < zs, 2 * p, 2 * (chips - 1 - p) + 1)

    place = place_of(chip)
    sibling = 2 * chip + 1 - core

    barrier = pltpu.get_barrier_semaphore()

    @pl.loop(1, n)
    def _(j):
        pl.semaphore_signal(
            barrier, inc=1, device_id={"dp": lax.rem(me + j, n)}, device_id_type=MESH
        )

    pl.semaphore_wait(barrier, n - 1)

    def push(phase, j, src, dst):
        return pltpu.make_async_remote_copy(
            src_ref=src,
            dst_ref=dst,
            send_sem=push_send.at[phase, j],
            recv_sem=push_recv.at[phase, j],
            device_id={"dp": lax.rem(me + j, n)},
            device_id_type=MESH,
        )

    def push_all(phase, src_of, dst):
        @pl.loop(1, n)
        def _(j):
            push(phase, j, src_of(lax.rem(me + j, n)), dst).start()

    def wait_all(phase, src_of, dst):
        @pl.loop(1, n)
        def _(j):
            push(phase, j, src_of(lax.rem(me + j, n)), dst).wait()

    last = chips // 2

    def part_of(idx, step, way):
        if step < last:
            return wd_all.at[idx]
        return wd_all.at[idx, pl.ds(way * half, half)]

    def source_place(step, way):
        return place - step if way == 0 else place + step

    def ring(step, way):
        target = place + 1 if way == 0 else place - 1
        origin = 2 * chip_at(source_place(step - 1, way)) + core
        return pltpu.make_async_remote_copy(
            src_ref=part_of(origin, step, way),
            dst_ref=part_of(origin, step, way),
            send_sem=ring_send.at[way, step],
            recv_sem=ring_recv.at[way, step],
            device_id={"dp": 2 * chip_at(target) + core},
            device_id_type=MESH,
        )

    def sib(step, way):
        origin = 2 * chip_at(source_place(step, way)) + core
        return pltpu.make_async_remote_copy(
            src_ref=part_of(origin, step, way),
            dst_ref=part_of(origin, step, way),
            send_sem=sib_send.at[way, step],
            recv_sem=sib_recv.at[way, step],
            device_id={"dp": sibling},
            device_id_type=MESH,
        )

    up_all[me] = upad_ref[...]
    push_all(0, lambda d: upad_ref, up_all.at[me])
    wd_all[me] = wd_ref[...]
    ring(1, 0).start()
    ring(1, 1).start()
    sib(0, 0).start()
    wait_all(0, lambda d: upad_ref, up_all.at[me])

    up_flat = up_all[...].reshape(n * PAD, left + tok)[:, :left]
    q = iota((cols, n * PAD), 1)
    r = iota((cols, n * PAD), 0)

    def spread_of(side):
        row = q % PAD - side * SIDE
        return onehot((row >= 0) & (row < up_rows) & ((q // PAD) * up_rows + row == r))

    spread = (spread_of(0), spread_of(1))
    up_full = jnp.concatenate([dot(m, up_flat).astype(bf16) for m in spread], axis=1)
    owner = iota((tok, cols), 1) // RANK
    back = dot(dv_ref[...], up_full, 1, 1)
    back = jnp.where(ra_col_ref[...] == owner, back, 0.0).astype(bf16)
    fold = onehot(iota((RANK, cols), 1) % RANK == iota((RANK, cols), 0))
    b_all[me] = dot(fold, back, 1, 1).astype(bf16)
    push_all(1, lambda d: b_all.at[me], b_all.at[me])
    dvb[:, :dv_width] = dv_ref[...]
    dvb[:, dv_width:] = (back.astype(f32) * adapter_scale).astype(bf16)
    acc[...] = jnp.zeros_like(acc)

    def work(p, k):
        d = 2 * chip_at(p) + k
        where = pl.ds(pl.multiple_of(d * depth, depth), depth)
        block = wd_all[d]
        acc[...] += dot(x_ref[:, where], block)
        ig_ref[:, where] = dot(dvb[...], block, 1, 1).astype(bf16)

    def step_on(step):
        for way in (0, 1):
            ring(step, way).wait_recv()
            if step < last:
                ring(step + 1, way).start()
            sib(step, way).start()

    step_on(1)
    work(place, core)

    wait_all(1, lambda d: b_all.at[me], b_all.at[me])
    pd_col = pd_col_ref[...]

    def pick(d, carry):
        rows, adapter = carry
        hit = pd_col == d * tok + iota((tok, tok), 1)
        rows = rows + dot(onehot(hit), b_all[d], 1, 1)
        ad = up_all[d][:1, left:].astype(f32)
        adapter = adapter + jnp.sum(jnp.where(hit, ad, 0.0), axis=1, keepdims=True)
        return rows, adapter

    home, adapter = lax.fori_loop(
        0, n, pick, (jnp.zeros((tok, RANK), f32), jnp.zeros((tok, 1), f32))
    )
    home = dot(home.astype(bf16), fold)
    home = jnp.where(adapter == owner.astype(f32), home, 0.0).astype(bf16)
    scale_factor = adapter_scale / (tok * n)

    @pl.loop(0, n)
    def _(d):
        where = pl.ds(pl.multiple_of(d * depth, depth), depth)
        c = d // 2
        grad[d % 2, c % 2, c // 2] = (
            dot(x_ref[:, where], home, 0, 0) * scale_factor
        ).astype(bf16)

    def pair(stage, src, dst, device):
        return pltpu.make_async_remote_copy(
            src_ref=src,
            dst_ref=dst,
            send_sem=pair_send.at[stage],
            recv_sem=pair_recv.at[stage],
            device_id={"dp": device},
            device_id_type=MESH,
        )

    over_core = pair(0, grad.at[1 - core], grad_core, sibling)
    over_y = pair(
        1, grad.at[core, 1 - my_y], grad_y, 2 * (2 * my_z + 1 - my_y) + core
    )

    def over_z(j):
        z = lax.rem(my_z + j, zs)
        return pltpu.make_async_remote_copy(
            src_ref=grad.at[core, my_y, z],
            dst_ref=grad_z.at[my_z],
            send_sem=z_send.at[j],
            recv_sem=z_recv.at[j],
            device_id={"dp": 2 * (2 * z + my_y) + core},
            device_id_type=MESH,
        )

    def start_y():
        over_core.wait()

        @pl.loop(0, 2 * zs)
        def _(i):
            y, z = i // zs, i % zs
            total = grad[core, y, z].astype(f32) + grad_core[y, z].astype(f32)
            grad[core, y, z] = total.astype(bf16)

        over_y.start()

    def start_z():
        over_y.wait()

        @pl.loop(0, zs)
        def _(z):
            total = grad[core, my_y, z].astype(f32) + grad_y[z].astype(f32)
            grad[core, my_y, z] = total.astype(bf16)

        @pl.loop(1, zs)
        def _(j):
            over_z(j).start()

        grad_z[my_z] = grad[core, my_y, my_z]

    over_core.start()
    sib(0, 0).wait_recv()
    work(place, 1 - core)
    start_y()
    for step in range(2, last + 1):
        step_on(step)
        if step == 2:
            start_z()
        for way in (0, 1):
            work(source_place(step - 1, way), core)
            sib(step - 1, way).wait_recv()
            work(source_place(step - 1, way), 1 - core)
    work(place + last, core)
    sib(last, 0).wait_recv()
    sib(last, 1).wait_recv()
    work(place + last, 1 - core)

    low = jnp.where(adapter == owner.astype(f32), acc[:, dv_width:], 0.0).astype(bf16)
    val = (acc[:, :dv_width] + adapter_scale * dot(low, up_full)).astype(bf16)
    tr = pd_row_ref[...] // tok
    same = (pd_col // tok == tr) & (iota((tok, tok), 0) < iota((tok, tok), 1))
    turn = jnp.sum(jnp.where(same, 1.0, 0.0), axis=0, keepdims=True).astype(i32)
    spot = tr * PAD + turn
    line = iota((n * PAD, tok), 0)
    order = (onehot(spot == line), onehot(spot + SIDE == line))
    slot = jnp.broadcast_to((pd_col % tok + 1).astype(f32), (tok, tok)).astype(bf16)
    for (first, second), lo, hi in (
        ((val[:, :left], val[:, left:]), 0, left),
        ((low, slot), left, left + tok),
    ):
        block = dot(order[0], first) + dot(order[1], second)
        v_send[:, :, lo:hi] = block.astype(bf16).reshape(n, PAD, hi - lo)
    push_all(3, lambda d: v_send.at[d], v_recv.at[me])
    v_recv[me] = v_send[me]

    @pl.loop(1, zs)
    def _(j):
        over_z(j).wait()

    gd_ref[...] = lax.fori_loop(
        0, zs, lambda z, s: s + grad_z[z].astype(f32), jnp.zeros(gd_ref.shape, f32)
    )

    wait_all(3, lambda d: v_send.at[d], v_recv.at[me])
    got = v_recv[...].reshape(n * PAD, left + tok)
    tag = v_recv[:, :, left:].astype(f32)
    tag_up = jnp.concatenate([tag[:, SIDE:], tag[:, :SIDE]], axis=1)
    wanted = (iota((n * PAD, tok), 1) + 1).astype(f32)
    upper = line % PAD < SIDE
    put_up = onehot(upper & (tag_up.reshape(n * PAD, tok) == wanted))
    put_down = onehot(jnp.logical_not(upper) & (tag.reshape(n * PAD, tok) == wanted))
    packed = dot(put_up, got, 0, 0).astype(bf16)
    values_ref[:, :left] = packed[:, :left]
    values_ref[:, left:] = dot(put_down, got[:, :left], 0, 0).astype(bf16)

    low_packed = packed[:, left:]
    low_wide = [dot(low_packed, m).astype(bf16) for m in spread]
    grad_up = dot(low_wide[0], dv_ref[:, :left], 0, 0)
    grad_up = (grad_up + dot(low_wide[1], dv_ref[:, left:], 0, 0)) * scale_factor
    u_send[...] = grad_up.astype(bf16).reshape(n, PAD, left)
    push_all(2, lambda d: u_send.at[d], u_recv.at[me])
    u_recv[me] = u_send[me]

    for way in (0, 1):
        for step in range(1, last + 1):
            ring(step, way).wait_send()
            sib(step, way).wait_send()
    sib(0, 0).wait_send()

    wait_all(2, lambda d: u_send.at[d], u_recv.at[me])
    gu_ref[...] = lax.fori_loop(
        0, n, lambda d, s: s + u_recv[d].astype(f32), jnp.zeros(gu_ref.shape, f32)
    )


def local(
    n,
    inputs,
    pack_dest,
    row_adapter,
    value_matrix,
    down_master,
    up_master,
    down_m,
    down_v,
    up_m,
    up_v,
    value_gradient,
):
    tok, width = inputs.shape
    depth, dv_width = value_matrix.shape
    cols = down_master.shape[1]
    up_rows = up_master.shape[0]
    wide = dv_width + cols
    wd = jnp.concatenate([value_matrix, down_master.astype(bf16)], axis=1)
    left = dv_width // 2
    up_b = up_master.astype(bf16)
    gap = ((0, SIDE - up_rows), (0, 0))
    halves = [jnp.pad(up_b[:, :left], gap), jnp.pad(up_b[:, left:], gap)]
    adapters = jnp.broadcast_to(row_adapter.astype(bf16)[None, :], (PAD, tok))
    upad = jnp.concatenate([jnp.concatenate(halves, axis=0), adapters], axis=1)
    steps = n // 4 + 1
    vmem = pl.BlockSpec(memory_space=pltpu.VMEM)
    values, input_gradient, grad_down, grad_up = pl.pallas_call(
        functools.partial(kernel, n, up_rows),
        out_shape=(
            jax.ShapeDtypeStruct((tok, dv_width), bf16),
            jax.ShapeDtypeStruct((tok, width), bf16),
            jax.ShapeDtypeStruct((depth, cols), f32),
            jax.ShapeDtypeStruct((PAD, left), f32),
        ),
        in_specs=[vmem] * 7,
        out_specs=[vmem] * 4,
        scratch_shapes=[
            pltpu.VMEM((n, depth, wide), bf16),
            pltpu.VMEM((n, PAD, left + tok), bf16),
            pltpu.VMEM((n, RANK, tok), bf16),
            pltpu.VMEM((2, 2, n // 4, depth, cols), bf16),
            pltpu.VMEM((2, n // 4, depth, cols), bf16),
            pltpu.VMEM((n // 4, depth, cols), bf16),
            pltpu.VMEM((n // 4, depth, cols), bf16),
            pltpu.VMEM((n, PAD, left + tok), bf16),
            pltpu.VMEM((n, PAD, left + tok), bf16),
            pltpu.VMEM((n, PAD, left), bf16),
            pltpu.VMEM((n, PAD, left), bf16),
            pltpu.VMEM((tok, wide), f32),
            pltpu.VMEM((tok, wide), bf16),
            pltpu.SemaphoreType.DMA((2, steps)),
            pltpu.SemaphoreType.DMA((2, steps)),
            pltpu.SemaphoreType.DMA((2, steps)),
            pltpu.SemaphoreType.DMA((2, steps)),
            pltpu.SemaphoreType.DMA((4, n)),
            pltpu.SemaphoreType.DMA((4, n)),
            pltpu.SemaphoreType.DMA((2,)),
            pltpu.SemaphoreType.DMA((2,)),
            pltpu.SemaphoreType.DMA((n // 4,)),
            pltpu.SemaphoreType.DMA((n // 4,)),
        ],
        compiler_params=pltpu.CompilerParams(
            collective_id=0, has_side_effects=True, vmem_limit_bytes=56 * 2**20
        ),
        cost_estimate=pl.CostEstimate(
            flops=6 * tok * width * wide,
            bytes_accessed=2 * (2 * tok * width + width * wide),
            transcendentals=0,
        ),
    )(
        inputs,
        pack_dest.reshape(tok, 1),
        pack_dest.reshape(1, tok),
        row_adapter.reshape(tok, 1),
        wd,
        upad,
        value_gradient,
    )
    grad_up = jnp.concatenate(
        [grad_up[:up_rows], grad_up[SIDE : SIDE + up_rows]], axis=1
    )
    new_down, new_down_m, new_down_v = adam_update(down_master, down_m, down_v, grad_down)
    new_up, new_up_m, new_up_v = adam_update(up_master, up_m, up_v, grad_up)
    return (values, input_gradient, new_down, new_down_m, new_down_v, new_up, new_up_m, new_up_v)


def solution(mesh):
    both = P(("group", "dp"), None)
    line = P(("group", "dp"))
    in_specs = (both, line, line, P("dp", None)) + (both,) * 7
    return jax.shard_map(
        functools.partial(local, mesh.shape["dp"]),
        mesh=mesh,
        in_specs=in_specs,
        out_specs=(both,) * 8,
        check_vma=False,
    )
```

```python
import functools

import jax
import jax.numpy as jnp
from jax import lax
from jax.experimental import pallas as pl
from jax.experimental.pallas import tpu as pltpu
from jax.sharding import PartitionSpec as P

RANK = 16
PAD = 16
SIDE = PAD // 2
MESH = pl.DeviceIdType.MESH

adapter_scale = 2.0
beta_one = 0.9
beta_two = 0.999
learn_rate = 0.001
adam_eps = 1e-08
first_fix = 1.0 - 0.9**10
second_fix = 1.0 - 0.999**10

bf16, f32, i32 = jnp.bfloat16, jnp.float32, jnp.int32


def adam_update(param, moment, second, gradient):
    moment_new = beta_one * moment + (1.0 - beta_one) * gradient
    second_new = beta_two * second + (1.0 - beta_two) * gradient * gradient
    param_new = param - learn_rate * (moment_new / first_fix) / (
        jnp.sqrt(second_new / second_fix) + adam_eps
    )
    return (param_new, moment_new, second_new)


def dot(left, right, lc=1, rc=0):
    return lax.dot_general(
        left, right, (((lc,), (rc,)), ((), ())), preferred_element_type=f32
    )


def iota(shape, dim):
    return lax.broadcasted_iota(i32, shape, dim)


def onehot(cond):
    return jnp.where(cond, 1.0, 0.0).astype(bf16)


def kernel(
    n,
    up_rows,
    x_ref,
    pd_col_ref,
    pd_row_ref,
    ra_col_ref,
    wd_ref,
    upad_ref,
    dv_ref,
    values_ref,
    ig_ref,
    gd_ref,
    gu_ref,
    wd_all,
    up_all,
    b_all,
    grad,
    grad_core,
    grad_y,
    grad_z,
    v_send,
    v_recv,
    u_send,
    u_recv,
    acc,
    dvb,
    ring_send,
    ring_recv,
    sib_send,
    sib_recv,
    push_send,
    push_recv,
    pair_send,
    pair_recv,
    z_send,
    z_recv,
    low_send,
    low_recv,
    x_send,
    x_recv,
):
    tok = x_ref.shape[0]
    depth, wide = wd_ref.shape
    dv_width = dv_ref.shape[1]
    cols = wide - dv_width
    chips = n // 2
    half = depth // 2
    group = lax.axis_index("group")
    mirror = group + 1 - 2 * lax.rem(group, 2)
    part = lax.rem(group, 2)
    me = lax.axis_index("dp")
    core = lax.rem(me, 2)
    chip = me // 2
    zs = chips // 2
    my_z, my_y = chip // 2, lax.rem(chip, 2)
    left = dv_width // 2

    def place_of(c):
        z, y = c // 2, lax.rem(c, 2)
        return jnp.where(y == 0, z, chips - 1 - z)

    def chip_at(p):
        p = lax.rem(p + chips, chips)
        return jnp.where(p < zs, 2 * p, 2 * (chips - 1 - p) + 1)

    place = place_of(chip)
    sibling = 2 * chip + 1 - core

    barrier = pltpu.get_barrier_semaphore()

    @pl.loop(1, n)
    def _(j):
        pl.semaphore_signal(
            barrier, inc=1, device_id={"dp": lax.rem(me + j, n)}, device_id_type=MESH
        )

    pl.semaphore_signal(barrier, inc=1, device_id={"group": mirror}, device_id_type=MESH)
    pl.semaphore_wait(barrier, n)

    def push(phase, j, src, dst):
        return pltpu.make_async_remote_copy(
            src_ref=src,
            dst_ref=dst,
            send_sem=push_send.at[phase, j],
            recv_sem=push_recv.at[phase, j],
            device_id={"dp": lax.rem(me + j, n)},
            device_id_type=MESH,
        )

    def push_all(phase, src_of, dst):
        @pl.loop(1, n)
        def _(j):
            push(phase, j, src_of(lax.rem(me + j, n)), dst).start()

    def wait_all(phase, src_of, dst):
        @pl.loop(1, n)
        def _(j):
            push(phase, j, src_of(lax.rem(me + j, n)), dst).wait()

    last = chips // 2

    def part_of(idx, step, way):
        if step < last:
            return wd_all.at[idx]
        return wd_all.at[idx, pl.ds(way * half, half)]

    def source_place(step, way):
        return place - step if way == 0 else place + step

    def frozen(idx, step, way):
        if step < 2:
            return wd_all.at[idx]
        if step < last:
            rows = pl.ds(pl.multiple_of(part * half, half), half)
        else:
            start = part * half + way * (half // 2)
            rows = pl.ds(pl.multiple_of(start, half // 2), half // 2)
        return wd_all.at[idx, rows, pl.ds(0, dv_width)]

    def to_next(ref, step, way, sends, recvs):
        target = place + 1 if way == 0 else place - 1
        return pltpu.make_async_remote_copy(
            src_ref=ref,
            dst_ref=ref,
            send_sem=sends.at[way, step],
            recv_sem=recvs.at[way, step],
            device_id={"dp": 2 * chip_at(target) + core},
            device_id_type=MESH,
        )

    def ring(step, way):
        origin = 2 * chip_at(source_place(step - 1, way)) + core
        return to_next(frozen(origin, step, way), step, way, ring_send, ring_recv)

    def ring_low(step, way):
        origin = 2 * chip_at(source_place(step - 1, way)) + core
        rows = pl.ds(0, depth) if step < last else pl.ds(way * half, half)
        ref = wd_all.at[origin, rows, pl.ds(dv_width, cols)]
        return to_next(ref, step, way, low_send, low_recv)

    def across(step, way):
        origin = 2 * chip_at(source_place(step, way)) + core
        ref = frozen(origin, step, way)
        return pltpu.make_async_remote_copy(
            src_ref=ref,
            dst_ref=ref,
            send_sem=x_send.at[way, step],
            recv_sem=x_recv.at[way, step],
            device_id={"group": mirror},
            device_id_type=MESH,
        )

    def sib(step, way):
        origin = 2 * chip_at(source_place(step, way)) + core
        return pltpu.make_async_remote_copy(
            src_ref=part_of(origin, step, way),
            dst_ref=part_of(origin, step, way),
            send_sem=sib_send.at[way, step],
            recv_sem=sib_recv.at[way, step],
            device_id={"dp": sibling},
            device_id_type=MESH,
        )

    up_all[me] = upad_ref[...]
    push_all(0, lambda d: upad_ref, up_all.at[me])
    wd_all[me] = wd_ref[...]
    ring(1, 0).start()
    ring(1, 1).start()
    sib(0, 0).start()
    wait_all(0, lambda d: upad_ref, up_all.at[me])

    up_flat = up_all[...].reshape(n * PAD, left + tok)[:, :left]
    q = iota((cols, n * PAD), 1)
    r = iota((cols, n * PAD), 0)

    def spread_of(side):
        row = q % PAD - side * SIDE
        return onehot((row >= 0) & (row < up_rows) & ((q // PAD) * up_rows + row == r))

    spread = (spread_of(0), spread_of(1))
    up_full = jnp.concatenate([dot(m, up_flat).astype(bf16) for m in spread], axis=1)
    owner = iota((tok, cols), 1) // RANK
    back = dot(dv_ref[...], up_full, 1, 1)
    back = jnp.where(ra_col_ref[...] == owner, back, 0.0).astype(bf16)
    fold = onehot(iota((RANK, cols), 1) % RANK == iota((RANK, cols), 0))
    b_all[me] = dot(fold, back, 1, 1).astype(bf16)
    push_all(1, lambda d: b_all.at[me], b_all.at[me])
    dvb[:, :dv_width] = dv_ref[...]
    dvb[:, dv_width:] = (back.astype(f32) * adapter_scale).astype(bf16)
    acc[...] = jnp.zeros_like(acc)

    def work(p, k):
        d = 2 * chip_at(p) + k
        where = pl.ds(pl.multiple_of(d * depth, depth), depth)
        block = wd_all[d]
        acc[...] += dot(x_ref[:, where], block)
        ig_ref[:, where] = dot(dvb[...], block, 1, 1).astype(bf16)

    def step_on(step):
        for way in (0, 1):
            ring(step, way).wait_recv()
            if step < last:
                ring(step + 1, way).start()
            if step < 2:
                sib(step, way).start()
            else:
                across(step, way).start()
                ring_low(step, way).wait_recv()
            if step < last:
                ring_low(step + 1, way).start()

    def complete(step, way):
        if step >= 2:
            across(step, way).wait_recv()
            sib(step, way).start()

    step_on(1)
    work(place, core)

    wait_all(1, lambda d: b_all.at[me], b_all.at[me])
    pd_col = pd_col_ref[...]

    def pick(d, carry):
        rows, adapter = carry
        hit = pd_col == d * tok + iota((tok, tok), 1)
        rows = rows + dot(onehot(hit), b_all[d], 1, 1)
        ad = up_all[d][:1, left:].astype(f32)
        adapter = adapter + jnp.sum(jnp.where(hit, ad, 0.0), axis=1, keepdims=True)
        return rows, adapter

    home, adapter = lax.fori_loop(
        0, n, pick, (jnp.zeros((tok, RANK), f32), jnp.zeros((tok, 1), f32))
    )
    home = dot(home.astype(bf16), fold)
    home = jnp.where(adapter == owner.astype(f32), home, 0.0).astype(bf16)
    scale_factor = adapter_scale / (tok * n)

    @pl.loop(0, n)
    def _(d):
        where = pl.ds(pl.multiple_of(d * depth, depth), depth)
        c = d // 2
        grad[d % 2, c % 2, c // 2] = (
            dot(x_ref[:, where], home, 0, 0) * scale_factor
        ).astype(bf16)

    def pair(stage, src, dst, device):
        return pltpu.make_async_remote_copy(
            src_ref=src,
            dst_ref=dst,
            send_sem=pair_send.at[stage],
            recv_sem=pair_recv.at[stage],
            device_id={"dp": device},
            device_id_type=MESH,
        )

    over_core = pair(0, grad.at[1 - core], grad_core, sibling)
    over_y = pair(
        1, grad.at[core, 1 - my_y], grad_y, 2 * (2 * my_z + 1 - my_y) + core
    )

    def over_z(j):
        z = lax.rem(my_z + j, zs)
        return pltpu.make_async_remote_copy(
            src_ref=grad.at[core, my_y, z],
            dst_ref=grad_z.at[my_z],
            send_sem=z_send.at[j],
            recv_sem=z_recv.at[j],
            device_id={"dp": 2 * (2 * z + my_y) + core},
            device_id_type=MESH,
        )

    def start_y():
        over_core.wait()

        @pl.loop(0, 2 * zs)
        def _(i):
            y, z = i // zs, i % zs
            total = grad[core, y, z].astype(f32) + grad_core[y, z].astype(f32)
            grad[core, y, z] = total.astype(bf16)

        over_y.start()

    def start_z():
        over_y.wait()

        @pl.loop(0, zs)
        def _(z):
            total = grad[core, my_y, z].astype(f32) + grad_y[z].astype(f32)
            grad[core, my_y, z] = total.astype(bf16)

        @pl.loop(1, zs)
        def _(j):
            over_z(j).start()

        grad_z[my_z] = grad[core, my_y, my_z]

    over_core.start()
    sib(0, 0).wait_recv()
    work(place, 1 - core)
    start_y()
    for step in range(2, last + 1):
        step_on(step)
        if step == 2:
            start_z()
        for way in (0, 1):
            complete(step - 1, way)
        for way in (0, 1):
            work(source_place(step - 1, way), core)
            sib(step - 1, way).wait_recv()
            work(source_place(step - 1, way), 1 - core)
    across(last, 0).wait_recv()
    across(last, 1).wait_recv()
    sib(last, 0).start()
    sib(last, 1).start()
    work(place + last, core)
    sib(last, 0).wait_recv()
    sib(last, 1).wait_recv()
    work(place + last, 1 - core)

    low = jnp.where(adapter == owner.astype(f32), acc[:, dv_width:], 0.0).astype(bf16)
    val = (acc[:, :dv_width] + adapter_scale * dot(low, up_full)).astype(bf16)
    tr = pd_row_ref[...] // tok
    same = (pd_col // tok == tr) & (iota((tok, tok), 0) < iota((tok, tok), 1))
    turn = jnp.sum(jnp.where(same, 1.0, 0.0), axis=0, keepdims=True).astype(i32)
    spot = tr * PAD + turn
    line = iota((n * PAD, tok), 0)
    order = (onehot(spot == line), onehot(spot + SIDE == line))
    slot = jnp.broadcast_to((pd_col % tok + 1).astype(f32), (tok, tok)).astype(bf16)
    for (first, second), lo, hi in (
        ((val[:, :left], val[:, left:]), 0, left),
        ((low, slot), left, left + tok),
    ):
        block = dot(order[0], first) + dot(order[1], second)
        v_send[:, :, lo:hi] = block.astype(bf16).reshape(n, PAD, hi - lo)
    push_all(3, lambda d: v_send.at[d], v_recv.at[me])
    v_recv[me] = v_send[me]

    @pl.loop(1, zs)
    def _(j):
        over_z(j).wait()

    gd_ref[...] = lax.fori_loop(
        0, zs, lambda z, s: s + grad_z[z].astype(f32), jnp.zeros(gd_ref.shape, f32)
    )

    wait_all(3, lambda d: v_send.at[d], v_recv.at[me])
    got = v_recv[...].reshape(n * PAD, left + tok)
    tag = v_recv[:, :, left:].astype(f32)
    tag_up = jnp.concatenate([tag[:, SIDE:], tag[:, :SIDE]], axis=1)
    wanted = (iota((n * PAD, tok), 1) + 1).astype(f32)
    upper = line % PAD < SIDE
    put_up = onehot(upper & (tag_up.reshape(n * PAD, tok) == wanted))
    put_down = onehot(jnp.logical_not(upper) & (tag.reshape(n * PAD, tok) == wanted))
    packed = dot(put_up, got, 0, 0).astype(bf16)
    values_ref[:, :left] = packed[:, :left]
    values_ref[:, left:] = dot(put_down, got[:, :left], 0, 0).astype(bf16)

    low_packed = packed[:, left:]
    low_wide = [dot(low_packed, m).astype(bf16) for m in spread]
    grad_up = dot(low_wide[0], dv_ref[:, :left], 0, 0)
    grad_up = (grad_up + dot(low_wide[1], dv_ref[:, left:], 0, 0)) * scale_factor
    u_send[...] = grad_up.astype(bf16).reshape(n, PAD, left)
    push_all(2, lambda d: u_send.at[d], u_recv.at[me])
    u_recv[me] = u_send[me]

    for way in (0, 1):
        for step in range(1, last + 1):
            ring(step, way).wait_send()
            if step >= 2:
                ring_low(step, way).wait_send()
                across(step, way).wait_send()
            sib(step, way).wait_send()
    sib(0, 0).wait_send()

    wait_all(2, lambda d: u_send.at[d], u_recv.at[me])
    gu_ref[...] = lax.fori_loop(
        0, n, lambda d, s: s + u_recv[d].astype(f32), jnp.zeros(gu_ref.shape, f32)
    )


def local(
    n,
    inputs,
    pack_dest,
    row_adapter,
    value_matrix,
    down_master,
    up_master,
    down_m,
    down_v,
    up_m,
    up_v,
    value_gradient,
):
    tok, width = inputs.shape
    depth, dv_width = value_matrix.shape
    cols = down_master.shape[1]
    up_rows = up_master.shape[0]
    wide = dv_width + cols
    wd = jnp.concatenate([value_matrix, down_master.astype(bf16)], axis=1)
    left = dv_width // 2
    up_b = up_master.astype(bf16)
    gap = ((0, SIDE - up_rows), (0, 0))
    halves = [jnp.pad(up_b[:, :left], gap), jnp.pad(up_b[:, left:], gap)]
    adapters = jnp.broadcast_to(row_adapter.astype(bf16)[None, :], (PAD, tok))
    upad = jnp.concatenate([jnp.concatenate(halves, axis=0), adapters], axis=1)
    steps = n // 4 + 1
    vmem = pl.BlockSpec(memory_space=pltpu.VMEM)
    values, input_gradient, grad_down, grad_up = pl.pallas_call(
        functools.partial(kernel, n, up_rows),
        out_shape=(
            jax.ShapeDtypeStruct((tok, dv_width), bf16),
            jax.ShapeDtypeStruct((tok, width), bf16),
            jax.ShapeDtypeStruct((depth, cols), f32),
            jax.ShapeDtypeStruct((PAD, left), f32),
        ),
        in_specs=[vmem] * 7,
        out_specs=[vmem] * 4,
        scratch_shapes=[
            pltpu.VMEM((n, depth, wide), bf16),
            pltpu.VMEM((n, PAD, left + tok), bf16),
            pltpu.VMEM((n, RANK, tok), bf16),
            pltpu.VMEM((2, 2, n // 4, depth, cols), bf16),
            pltpu.VMEM((2, n // 4, depth, cols), bf16),
            pltpu.VMEM((n // 4, depth, cols), bf16),
            pltpu.VMEM((n // 4, depth, cols), bf16),
            pltpu.VMEM((n, PAD, left + tok), bf16),
            pltpu.VMEM((n, PAD, left + tok), bf16),
            pltpu.VMEM((n, PAD, left), bf16),
            pltpu.VMEM((n, PAD, left), bf16),
            pltpu.VMEM((tok, wide), f32),
            pltpu.VMEM((tok, wide), bf16),
            pltpu.SemaphoreType.DMA((2, steps)),
            pltpu.SemaphoreType.DMA((2, steps)),
            pltpu.SemaphoreType.DMA((2, steps)),
            pltpu.SemaphoreType.DMA((2, steps)),
            pltpu.SemaphoreType.DMA((4, n)),
            pltpu.SemaphoreType.DMA((4, n)),
            pltpu.SemaphoreType.DMA((2,)),
            pltpu.SemaphoreType.DMA((2,)),
            pltpu.SemaphoreType.DMA((n // 4,)),
            pltpu.SemaphoreType.DMA((n // 4,)),
            pltpu.SemaphoreType.DMA((2, steps)),
            pltpu.SemaphoreType.DMA((2, steps)),
            pltpu.SemaphoreType.DMA((2, steps)),
            pltpu.SemaphoreType.DMA((2, steps)),
        ],
        compiler_params=pltpu.CompilerParams(
            collective_id=0, has_side_effects=True, vmem_limit_bytes=56 * 2**20
        ),
        cost_estimate=pl.CostEstimate(
            flops=6 * tok * width * wide,
            bytes_accessed=2 * (2 * tok * width + width * wide),
            transcendentals=0,
        ),
    )(
        inputs,
        pack_dest.reshape(tok, 1),
        pack_dest.reshape(1, tok),
        row_adapter.reshape(tok, 1),
        wd,
        upad,
        value_gradient,
    )
    grad_up = jnp.concatenate(
        [grad_up[:up_rows], grad_up[SIDE : SIDE + up_rows]], axis=1
    )
    new_down, new_down_m, new_down_v = adam_update(down_master, down_m, down_v, grad_down)
    new_up, new_up_m, new_up_v = adam_update(up_master, up_m, up_v, grad_up)
    return (values, input_gradient, new_down, new_down_m, new_down_v, new_up, new_up_m, new_up_v)


def solution(mesh):
    both = P(("group", "dp"), None)
    line = P(("group", "dp"))
    in_specs = (both, line, line, P("dp", None)) + (both,) * 7
    return jax.shard_map(
        functools.partial(local, mesh.shape["dp"]),
        mesh=mesh,
        in_specs=in_specs,
        out_specs=(both,) * 8,
        check_vma=False,
    )
```
